128 devices in a mesh: occ: 4 (over y_hi, core), virt: 32 (over x, y_lo, z).
Axes of the slice: x: 4, y: 4 (y_hi: 2, y_lo: 2; y = y_hi * 2 + y_lo), z: 4, core: 2. Of those that a mesh axis runs over, the one named last changes fastest.
Arguments:
- factors: bfloat16 [2400, 640, 640], P('virt', 'occ'), may hold values from -0.25 to 0.25
- amplitudes: bfloat16 [16, 16, 2, 640], P('occ', None, None, 'virt'), may hold values from -6 to 6
- block_sizes: int32 [8], replicated, may hold values from 1 to 80, 600 in all
Outputs:
- residual: bfloat16 [16, 16, 640, 640], P('occ', None, None, 'virt')
The draws below stay inside these ranges and needn't reach their ends.
Inputs may be any that keep to these rules, and one draw needn't show every extreme that they name: `block_sizes`: the 8 entries sum to 600, and the largest equals 80.
All inputs are finite; a program needn't handle non-finite values.
Results may differ from the reference program's by a relative error of at most 0.0059.
Values may be sent and summed in bfloat16 or wider, within the bound.
No kernel may reach another device: no remote copies, remote signals or barrier semaphores. Data moves between devices by JAX's collectives and lax.ppermute only.
A program may use at most 192 MiB of HBM per device.

```python
import math
import jax
import jax.numpy as jnp
import numpy as np
from jax import lax

NVIRT = 600
IRREPS = 8
VBLOCK = 80
VIRTUAL_PADDED = 640
FITTING_COUNT = 2400
VIRTUAL_WINDOW = 2
OCCUPIED_WINDOW = 16


def block_levels(rng, shape, pieces, least, largest):
    def one(dim, shards_of):
        steps = jax.random.uniform(jax.random.fold_in(jax.random.fold_in(rng, 6), dim), (shards_of,), jnp.float32, least / len(pieces), largest / len(pieces))
        return jnp.repeat(jnp.exp(steps), shape[dim] // shards_of).reshape((-1,) + (1,) * (len(shape) - dim - 1))

    gain = one(*pieces[0])
    for cut in pieces[1:]:
        gain = gain * one(*cut)
    return gain


def profile(number_of, total, limit, slope):
    loads = [(1 << 20) // math.isqrt(grade ** slope) + 1 for grade in range(2, number_of + 1)]
    surplus, counts = total - limit - (number_of - 1), [1] * (number_of - 1)
    while surplus > 0:
        movable = [i for i in range(number_of - 1) if counts[i] < limit]
        pool, remaining = sum([loads[i] for i in movable]), surplus
        for i in movable:
            more = min(limit - counts[i], max(1, remaining * loads[i] // pool), surplus)
            counts[i] = counts[i] + more
            surplus = surplus - more
    return np.array([limit] + counts)


def uneven_parts(stream_key, amount, total, most, skew):
    if amount == 2:
        one = jax.random.randint(stream_key, (), max(1, total - most), min(most, total - 1) + 1)
        return jnp.stack([one, total - one])
    sizes = jnp.asarray(profile(amount, total, most, skew), jnp.int32)
    pairs = (amount - 1) // 2
    source_of, receiver = sizes[1:1 + 2 * pairs:2], sizes[2:2 + 2 * pairs:2]
    slack = jnp.minimum(source_of - 1, most - receiver)
    moved = jax.random.randint(jax.random.fold_in(stream_key, 1), (pairs,), 0, 1 << 20) % (slack + 1)
    sizes = sizes.at[1:1 + 2 * pairs:2].set(source_of - moved).at[2:2 + 2 * pairs:2].set(receiver + moved)
    return sizes[jax.random.permutation(jax.random.fold_in(stream_key, 2), amount)]


def bell_draw(rng, shape, width, most, shards=(), held_as=jnp.bfloat16):
    array = width * jax.random.normal(rng, shape, jnp.float32)
    if shards:
        array = array * block_levels(rng, shape, shards, -0.22, 0.18)
    return jnp.clip(array, -most, most).astype(held_as)


def setup_inputs(seed: int = 0) -> dict:
    streams_of = jax.random.split(jax.random.key(seed), 4)
    factors = bell_draw(streams_of[0], (FITTING_COUNT, VIRTUAL_PADDED, VIRTUAL_PADDED), VIRTUAL_PADDED ** -0.5, 0.25, ((0, 32), (1, 4)))
    amplitudes = bell_draw(streams_of[1], (OCCUPIED_WINDOW, OCCUPIED_WINDOW, VIRTUAL_WINDOW, VIRTUAL_PADDED), 1.0, 6.0, ((0, 4), (3, 32)))
    block_sizes = uneven_parts(streams_of[2], IRREPS, NVIRT, VBLOCK, 1).astype(jnp.int32)
    return {"factors": factors, "amplitudes": amplitudes, "block_sizes": block_sizes}


def usable_mask(block_sizes):
    position = jnp.arange(IRREPS * VBLOCK, dtype=jnp.int32)
    size_at = block_sizes[(position // VBLOCK).astype(jnp.int32)]
    return (position % VBLOCK) < size_at


def reference(factors, amplitudes, block_sizes):
    usable = usable_mask(block_sizes)
    keep = (usable[:VIRTUAL_WINDOW][:, None] & usable[None, :]).astype(jnp.bfloat16)
    masked = amplitudes * keep[None, None]
    masked_wide = masked.astype(jnp.float32)
    antisym = (masked_wide - jnp.transpose(masked_wide, (1, 0, 2, 3))).astype(jnp.bfloat16)
    window_columns = jnp.transpose(factors[:, :, :VIRTUAL_WINDOW], (2, 0, 1)).astype(jnp.float32)
    window_columns = window_columns.reshape(VIRTUAL_WINDOW * FITTING_COUNT, VIRTUAL_PADDED)
    flattened_factors = factors.reshape(FITTING_COUNT * VIRTUAL_PADDED, VIRTUAL_PADDED)

    def one_row(amplitude_row):
        left_operand = jnp.transpose(amplitude_row, (1, 0, 2)).reshape(VIRTUAL_WINDOW * OCCUPIED_WINDOW, VIRTUAL_PADDED)
        middle_operand = lax.dot_general(left_operand, flattened_factors, (((1,), (1,)), ((), ())), preferred_element_type=jnp.float32)
        middle_operand = lax.optimization_barrier(middle_operand.astype(jnp.bfloat16)).astype(jnp.float32)
        middle_operand = middle_operand.reshape(VIRTUAL_WINDOW, OCCUPIED_WINDOW, FITTING_COUNT, VIRTUAL_PADDED).transpose(0, 2, 1, 3).reshape(VIRTUAL_WINDOW * FITTING_COUNT, OCCUPIED_WINDOW, VIRTUAL_PADDED)
        return jnp.einsum("xa,xjb->jab", window_columns, middle_operand, precision=lax.Precision.HIGHEST)

    ladder = lax.map(one_row, antisym)
    outer = (usable[:, None] & usable[None, :]).astype(jnp.float32)
    return (ladder * outer[None, None]).astype(jnp.bfloat16)
```

```python
import functools

import jax
import jax.numpy as jnp
import numpy as np
from jax import lax
from jax.experimental import pallas as pl
from jax.experimental.pallas import tpu as pltpu
from jax.sharding import Mesh, PartitionSpec as P

OCC = ("yh", "core")
TILE = ("yl", "z", "x")
NPAIR = 128
QPAD = 80


def pair_tables(occ, cwin, occ_shards):
    pairs = [(i, j) for i in range(occ) for j in range(i + 1, occ)]
    per = occ // occ_shards
    pick = np.zeros((occ_shards, cwin, per, occ, cwin, NPAIR), np.float32)
    spread = np.zeros((occ, occ, NPAIR), np.float32)
    for p, (i, j) in enumerate(pairs):
        for c in range(cwin):
            pick[i // per, c, i % per, j, c, p] = 1.0
            pick[j // per, c, j % per, i, c, p] = -1.0
        spread[i, j, p] = 1.0
        spread[j, i, p] = -1.0
    return (
        pick.reshape(occ_shards, cwin * per * occ, cwin * NPAIR),
        spread.reshape(occ * occ, NPAIR),
    )


def share(x, axes, count):
    return lax.all_to_all(
        jnp.broadcast_to(x[None], (count,) + x.shape), axes, 0, 0, tiled=True
    )


def middle_kernel(q_local, dests, width, b_ref, a_ref, out_ref):
    step = pl.program_id(0)
    rows, b_local, v = b_ref.shape
    cwin = a_ref.shape[1] // NPAIR
    res = lax.dot_general(
        b_ref[...].reshape(rows * b_local, v),
        a_ref[...],
        (((1,), (0,)), ((), ())),
        preferred_element_type=jnp.float32,
    ).reshape(rows, b_local, cwin * NPAIR)
    q = step * rows + lax.broadcasted_iota(jnp.int32, (rows, 1, 1), 0)
    res = jnp.where(q < q_local, res, 0.0)
    res = jnp.swapaxes(res, 0, 1).astype(jnp.bfloat16)
    res = res.reshape(dests, width, rows, cwin * NPAIR)
    for c in range(cwin):
        for h in range(width):
            out_ref[:, c, :, h * NPAIR : (h + 1) * NPAIR] = res[
                :, h, :, c * NPAIR : (c + 1) * NPAIR
            ]


def middle(factors, amps, dests, width):
    q_local, b_local, v = factors.shape
    cwin = amps.shape[1] // NPAIR
    rows = 16
    return pl.pallas_call(
        functools.partial(middle_kernel, q_local, dests, width),
        grid=(QPAD // rows,),
        in_specs=[
            pl.BlockSpec((rows, b_local, v), lambda s: (s, 0, 0)),
            pl.BlockSpec(amps.shape, lambda s: (0, 0)),
        ],
        out_specs=pl.BlockSpec(
            (dests, cwin, rows, width * NPAIR), lambda s: (0, 0, s, 0)
        ),
        out_shape=jax.ShapeDtypeStruct(
            (dests, cwin, QPAD, width * NPAIR), jnp.bfloat16
        ),
        compiler_params=pltpu.CompilerParams(vmem_limit_bytes=48 << 20),
        cost_estimate=pl.CostEstimate(
            flops=2 * q_local * b_local * v * cwin * NPAIR,
            bytes_accessed=2 * (factors.size + dests * cwin * QPAD * width * NPAIR),
            transcendentals=0,
        ),
    )(factors, amps)


def per_device(factors, amplitudes, block_sizes):
    q_local, b_local, v = factors.shape
    occ_local, occ, cwin, tile = amplitudes.shape
    occ_shards, shards = occ // occ_local, v // tile
    nx = 4
    width = tile // nx
    irreps = block_sizes.shape[0]
    block = v // irreps
    pick_np, spread_np = pair_tables(occ, cwin, occ_shards)

    position = jnp.arange(v, dtype=jnp.int32)
    onehot = (position // block)[:, None] == jnp.arange(irreps, dtype=jnp.int32)[None, :]
    size_at = jnp.sum(jnp.where(onehot, block_sizes[None, :], 0), axis=1)
    usable = position % block < size_at

    own = jnp.transpose(amplitudes, (3, 2, 0, 1)).reshape(tile, cwin * occ_local * occ)
    every = share(own, OCC + ("x", "yl", "z"), occ_shards * shards)
    every = every.reshape(occ_shards, v, cwin * occ_local * occ)
    antisym = jnp.einsum(
        "odl,olm->dm",
        every,
        jnp.asarray(pick_np, jnp.bfloat16),
        preferred_element_type=jnp.float32,
    )
    keep = usable[:, None] & jnp.repeat(usable[:cwin], NPAIR)[None, :]
    antisym = jnp.where(keep, antisym, 0.0).astype(jnp.bfloat16)

    cols = jnp.transpose(factors[:, :, :cwin], (2, 0, 1))
    cols = jnp.pad(cols, ((0, 0), (0, QPAD - q_local), (0, 0)))
    cols = share(cols, OCC, occ_shards)
    cols = jnp.transpose(cols, (1, 2, 0, 3)).reshape(cwin, QPAD, v)
    half = lax.dynamic_index_in_dim(cols, lax.axis_index("core"), 0, keepdims=False)
    half = share(half, TILE, shards).reshape(shards, QPAD, v)
    columns = lax.all_gather(half, "core", axis=0, tiled=False)
    columns = jnp.transpose(columns, (1, 0, 2, 3)).reshape(shards * cwin * QPAD, v)

    mid = middle(factors, antisym, shards, width)
    mid = mid.reshape(shards, cwin * QPAD, width * NPAIR)
    tiles = lax.all_to_all(mid, TILE, 0, 0, tiled=True)
    tiles = tiles.reshape(shards * cwin * QPAD, width * NPAIR)
    ladder = lax.dot_general(
        tiles, columns, (((0,), (0,)), ((), ())), preferred_element_type=jnp.float32
    ).reshape(width, NPAIR, v)

    occ_at = lax.axis_index(OCC)
    x_at = lax.axis_index("x")
    tile_at = lax.axis_index(("yl", "z"))
    b_first = occ_at * b_local + tile_at * tile + x_at * width
    usable_b = lax.dynamic_slice_in_dim(usable, b_first, width)
    outer = usable_b[:, None, None] & usable[None, None, :]
    ladder = jnp.where(outer, ladder, 0.0).astype(jnp.bfloat16)
    spread = spread_np.reshape(occ_shards, occ_local, occ, NPAIR)
    rows = jnp.einsum(
        "oijp,hpa->oihja",
        jnp.asarray(spread, jnp.bfloat16),
        ladder,
        preferred_element_type=jnp.float32,
    ).astype(jnp.bfloat16)

    out = jnp.zeros((occ_local, nx, width, occ, v), jnp.bfloat16)
    for r in range(nx):
        perm = [
            (o * nx + x, ((x + r) % nx) * nx + o)
            for o in range(occ_shards)
            for x in range(nx)
        ]
        part = lax.dynamic_index_in_dim(rows, (x_at + r) % nx, 0, keepdims=False)
        part = lax.ppermute(part, OCC + ("x",), perm)
        out = lax.dynamic_update_slice(
            out, part[:, None], (0, (occ_at - r + nx) % nx, 0, 0, 0)
        )
    out = out.reshape(occ_local, nx * width, occ, v)
    return jnp.transpose(out, (0, 2, 3, 1))


def solution(mesh):
    split = Mesh(
        mesh.devices.reshape(2, 2, 4, 2, 4), ("yh", "core", "x", "yl", "z")
    )
    virt = ("x", "yl", "z")
    return jax.shard_map(
        per_device,
        mesh=split,
        in_specs=(P(virt, OCC, None), P(OCC, None, None, virt), P()),
        out_specs=P(OCC, None, None, virt),
        check_vma=False,
    )
```

```python
import functools

import jax
import jax.numpy as jnp
import numpy as np
from jax import lax
from jax.experimental import pallas as pl
from jax.experimental.pallas import tpu as pltpu
from jax.sharding import Mesh, PartitionSpec as P

OCC = ("yh", "core")
TILE = ("yl", "z", "x")
NPAIR = 128
QPAD = 80
WIDTHS = (3, 2)


def pair_tables(occ, cwin, occ_shards):
    pairs = [(i, j) for i in range(occ) for j in range(i + 1, occ)]
    per = occ // occ_shards
    pick = np.zeros((occ_shards, cwin, per, occ, cwin, NPAIR), np.float32)
    spread = np.zeros((occ, occ, NPAIR), np.float32)
    for p, (i, j) in enumerate(pairs):
        for c in range(cwin):
            pick[i // per, c, i % per, j, c, p] = 1.0
            pick[j // per, c, j % per, i, c, p] = -1.0
        spread[i, j, p] = 1.0
        spread[j, i, p] = -1.0
    return (
        pick.reshape(occ_shards, cwin * per * occ, cwin * NPAIR),
        spread.reshape(occ * occ, NPAIR),
    )


def share(x, axes, count):
    return lax.all_to_all(
        jnp.broadcast_to(x[None], (count,) + x.shape), axes, 0, 0, tiled=True
    )


def middle_kernel(q_local, dests, widths, b_ref, a_ref, *out_refs):
    step = pl.program_id(0)
    rows, b_local, v = b_ref.shape
    cwin = a_ref.shape[1] // NPAIR
    res = lax.dot_general(
        b_ref[...].reshape(rows * b_local, v),
        a_ref[...],
        (((1,), (0,)), ((), ())),
        preferred_element_type=jnp.float32,
    ).reshape(rows, b_local, cwin * NPAIR)
    q = step * rows + lax.broadcasted_iota(jnp.int32, (rows, 1, 1), 0)
    res = jnp.where(q < q_local, res, 0.0)
    res = jnp.swapaxes(res, 0, 1).astype(jnp.bfloat16)
    res = res.reshape(dests, sum(widths), rows, cwin * NPAIR)
    first = 0
    for out_ref, width in zip(out_refs, widths):
        for c in range(cwin):
            for h in range(width):
                out_ref[:, c, :, h * NPAIR : (h + 1) * NPAIR] = res[
                    :, first + h, :, c * NPAIR : (c + 1) * NPAIR
                ]
        first += width


def middle(factors, amps, dests, widths):
    q_local, b_local, v = factors.shape
    cwin = amps.shape[1] // NPAIR
    rows = 16
    width = sum(widths)
    return pl.pallas_call(
        functools.partial(middle_kernel, q_local, dests, widths),
        grid=(QPAD // rows,),
        in_specs=[
            pl.BlockSpec((rows, b_local, v), lambda s: (s, 0, 0)),
            pl.BlockSpec(amps.shape, lambda s: (0, 0)),
        ],
        out_specs=[
            pl.BlockSpec((dests, cwin, rows, w * NPAIR), lambda s: (0, 0, s, 0))
            for w in widths
        ],
        out_shape=[
            jax.ShapeDtypeStruct((dests, cwin, QPAD, w * NPAIR), jnp.bfloat16)
            for w in widths
        ],
        compiler_params=pltpu.CompilerParams(vmem_limit_bytes=48 << 20),
        cost_estimate=pl.CostEstimate(
            flops=2 * q_local * b_local * v * cwin * NPAIR,
            bytes_accessed=2 * (factors.size + dests * cwin * QPAD * width * NPAIR),
            transcendentals=0,
        ),
    )(factors, amps)


def column_kernel(at_ref, *refs):
    pieces, out_ref = refs[:-1], refs[-1]
    occ_at, core_at = at_ref[0], at_ref[1]
    count = len(pieces)
    a_part = pieces[0].shape[2]
    own = [ref[core_at] for ref in pieces]
    for p in range(count):
        k = lax.rem(occ_at - p + count, count)
        value = own[0]
        for n in range(1, count):
            value = jnp.where(k == n, own[n], value)
        out_ref[:, :, p * a_part : (p + 1) * a_part] = jnp.broadcast_to(
            value[None], (out_ref.shape[0],) + value.shape
        )


def column_copies(pieces, at, copies):
    _, depth, a_part = pieces[0].shape
    vmem = pl.BlockSpec(memory_space=pltpu.VMEM)
    return pl.pallas_call(
        column_kernel,
        in_specs=[pl.BlockSpec(memory_space=pltpu.SMEM)] + [vmem] * len(pieces),
        out_specs=vmem,
        out_shape=jax.ShapeDtypeStruct(
            (copies, depth, len(pieces) * a_part), jnp.bfloat16
        ),
        compiler_params=pltpu.CompilerParams(vmem_limit_bytes=16 << 20),
    )(at, *pieces)


def ladder_kernel(
    groups, at_ref, m_ref, w_own_ref, w_far_ref, keep_ref, spread_ref, *refs
):
    outs, acc = refs[:-1], refs[-1]
    step, last = pl.program_id(0), pl.num_programs(0) - 1
    depth = m_ref.shape[0] * m_ref.shape[2]
    width = acc.shape[1] // NPAIR
    occ_local, occ = outs[0].shape[0], outs[0].shape[2]

    @pl.when(step == 0)
    def _():
        acc[...] = jnp.zeros_like(acc)

    def add(w_ref):
        acc[...] += jnp.dot(
            w_ref[...],
            m_ref[...].reshape(depth, -1),
            preferred_element_type=jnp.float32,
        )

    pl.when(step < groups)(lambda: add(w_own_ref))
    pl.when(step >= groups)(lambda: add(w_far_ref))

    @pl.when(step == last)
    def _():
        for h in range(width):
            part = acc[:, h * NPAIR : (h + 1) * NPAIR].astype(jnp.bfloat16)
            rows = lax.dot_general(
                spread_ref[...],
                part,
                (((1,), (1,)), ((), ())),
                preferred_element_type=jnp.float32,
            )
            rows = (rows * keep_ref[h : h + 1, :]).astype(jnp.bfloat16)
            rows = rows.reshape(len(outs), occ_local, occ, -1)
            for r, out in enumerate(outs):
                out[:, h] = rows[r]


def ladder_rows(tiles, own, far, keep, spread, at, occ_local, occ):
    _, sources, _, depth, lanes = tiles.shape
    a_size = own.shape[1]
    groups = 2
    width = lanes // NPAIR
    shards = occ // occ_local

    def m_at(s, at):
        yl = (at[0] + s % groups) % 2
        c = (at[1] + s // groups) % 2
        return yl, 0, c, 0, 0

    own_at = lambda s, at: (jnp.minimum(s, groups - 1), 0, 0)
    far_at = lambda s, at: (jnp.maximum(s - groups, 0), 0, 0)

    out_block = (occ_local, width, occ, a_size)
    whole = lambda n: lambda s, at: (0,) * n
    return pl.pallas_call(
        functools.partial(ladder_kernel, groups),
        grid_spec=pltpu.PrefetchScalarGridSpec(
            num_scalar_prefetch=1,
            grid=(2 * groups,),
            in_specs=[
                pl.BlockSpec((None, sources, 1, depth, lanes), m_at),
                pl.BlockSpec((None, a_size, sources * depth), own_at),
                pl.BlockSpec((None, a_size, sources * depth), far_at),
                pl.BlockSpec(keep.shape, whole(2)),
                pl.BlockSpec(spread.shape, whole(2)),
            ],
            out_specs=[pl.BlockSpec(out_block, whole(4))] * shards,
            scratch_shapes=[pltpu.VMEM((a_size, lanes), jnp.float32)],
        ),
        out_shape=[jax.ShapeDtypeStruct(out_block, jnp.bfloat16)] * shards,
        compiler_params=pltpu.CompilerParams(vmem_limit_bytes=48 << 20),
        cost_estimate=pl.CostEstimate(
            flops=2 * tiles.size * a_size,
            bytes_accessed=2 * (tiles.size + own.size + far.size),
            transcendentals=0,
        ),
    )(at, tiles, own, far, keep, spread)


def per_device(factors, amplitudes, block_sizes):
    q_local, b_local, v = factors.shape
    occ_local, occ, cwin, tile = amplitudes.shape
    occ_shards, shards = occ // occ_local, v // tile
    nx = lax.axis_size("x")
    width = tile // nx
    irreps = block_sizes.shape[0]
    block = v // irreps
    pick_np, spread_np = pair_tables(occ, cwin, occ_shards)
    occ_at, x_at, core_at = (lax.axis_index(n) for n in (OCC, "x", "core"))

    position = jnp.arange(v, dtype=jnp.int32)
    onehot = (position // block)[:, None] == jnp.arange(irreps, dtype=jnp.int32)[None, :]
    size_at = jnp.sum(jnp.where(onehot, block_sizes[None, :], 0), axis=1)
    usable = position % block < size_at

    own = jnp.transpose(amplitudes, (3, 2, 0, 1)).reshape(tile, cwin * occ_local * occ)
    every = share(own, OCC + ("x", "yl", "z"), occ_shards * shards)
    every = every.reshape(occ_shards, v, cwin * occ_local * occ)
    antisym = jnp.einsum(
        "odl,olm->dm",
        every,
        jnp.asarray(pick_np, jnp.bfloat16),
        preferred_element_type=jnp.float32,
    )
    keep = usable[:, None] & jnp.repeat(usable[:cwin], NPAIR)[None, :]
    antisym = jnp.where(keep, antisym, 0.0).astype(jnp.bfloat16)

    cols = jnp.transpose(factors[:, :, :cwin], (2, 0, 1))
    cols = jnp.pad(cols, ((0, 0), (0, QPAD - q_local), (0, 0)))
    pieces = [cols]
    for k in range(1, occ_shards):
        shift = [(o, (o + k) % occ_shards) for o in range(occ_shards)]
        pieces.append(lax.ppermute(cols, OCC, shift))
    sources = shards // 2
    where = jnp.stack([occ_at, core_at]).astype(jnp.int32)
    half = column_copies(pieces, where, sources)
    half = lax.all_to_all(half, TILE[1:], 0, 0, tiled=True)
    half, mids = lax.optimization_barrier(
        (half, middle(factors, antisym, shards, WIDTHS))
    )
    half = half.reshape(sources * QPAD, v).T
    swap_y = [(0, 3), (3, 0), (1, 2), (2, 1)]
    other = lax.ppermute(half, ("yh", "yl"), swap_y)
    own_cols = jnp.stack([half, other])
    far_cols = lax.ppermute(own_cols, "core", [(0, 1), (1, 0)])

    tile_at = lax.axis_index(("yl", "z"))
    b_first = occ_at * b_local + tile_at * tile + x_at * width
    usable_b = lax.dynamic_slice_in_dim(usable, b_first, width)
    outer = (usable_b[:, None] & usable[None, :]).astype(jnp.float32)
    spread = jnp.asarray(np.concatenate([spread_np, spread_np]), jnp.bfloat16)
    rows_per = occ_local * occ
    spread = lax.dynamic_slice_in_dim(spread, x_at * rows_per, occ * occ)
    at = jnp.stack([lax.axis_index("yl"), core_at]).astype(jnp.int32)

    first, tiles, parts, landed = 0, None, None, []
    for mid, w in zip(mids, WIDTHS):
        mid = mid.reshape(shards, cwin * QPAD, w * NPAIR)
        if tiles is not None:
            tiles, mid = lax.optimization_barrier((tiles, mid))
        tiles = lax.all_to_all(mid, TILE, 0, 0, tiled=True)
        if parts is not None:
            tiles, parts = lax.optimization_barrier((tiles, parts))
        keep = jnp.pad(outer[first : first + w], ((0, -w % 8), (0, 0)))
        parts = ladder_rows(
            tiles.reshape(2, sources, cwin, QPAD, w * NPAIR),
            own_cols, far_cols, keep, spread, at, occ_local, occ,
        )
        if landed:
            arrived, parts = lax.optimization_barrier(
                ([part for part, _, _ in landed], parts)
            )
            landed = [(p,) + old[1:] for p, old in zip(arrived, landed)]
        for r in range(nx):
            perm = [
                (o * nx + x, ((x + r) % nx) * nx + o)
                for o in range(occ_shards)
                for x in range(nx)
            ]
            part = lax.ppermute(parts[r], OCC + ("x",), perm)
            landed.append((part, (occ_at - r + nx) % nx, first))
        first += w
    out = jnp.zeros((occ_local, nx, width, occ, v), jnp.bfloat16)
    for part, x_from, first in landed:
        out = lax.dynamic_update_slice(out, part[:, None], (0, x_from, first, 0, 0))
    out = out.reshape(occ_local, nx * width, occ, v)
    return jnp.transpose(out, (0, 2, 3, 1))


def solution(mesh):
    split = Mesh(
        mesh.devices.reshape(2, 2, 4, 2, 4), ("yh", "core", "x", "yl", "z")
    )
    virt = ("x", "yl", "z")
    return jax.shard_map(
        per_device,
        mesh=split,
        in_specs=(P(virt, OCC, None), P(OCC, None, None, virt), P()),
        out_specs=P(OCC, None, None, virt),
        check_vma=False,
    )
```

```python
import functools

import jax
import jax.numpy as jnp
import numpy as np
from jax import lax
from jax.experimental import pallas as pl
from jax.experimental.pallas import tpu as pltpu
from jax.sharding import Mesh, PartitionSpec as P

OCC = ("yh", "core")
TILE = ("yl", "z", "x")
NPAIR = 128
OWNED = 56
QPAD = 80
WIDTHS = (4, 1)


def pair_tables(occ, cwin, occ_shards):
    pairs = [(i, j) for i in range(occ) for j in range(i + 1, occ)]
    per = occ // occ_shards
    pick = np.zeros((occ_shards, cwin, per, occ, cwin, NPAIR), np.float32)
    select = np.zeros((occ_shards, OWNED, NPAIR), np.float32)
    spread = np.zeros((occ_shards, per, occ, OWNED), np.float32)
    count = [0] * occ_shards
    for p, (i, j) in enumerate(pairs):
        for c in range(cwin):
            pick[i // per, c, i % per, j, c, p] = 1.0
            pick[j // per, c, j % per, i, c, p] = -1.0
        for o in sorted({i // per, j // per}):
            n = count[o]
            count[o] += 1
            select[o, n, p] = 1.0
            if i // per == o:
                spread[o, i % per, j, n] = 1.0
            if j // per == o:
                spread[o, j % per, i, n] = -1.0
    return (
        pick.reshape(occ_shards, cwin * per * occ, cwin * NPAIR),
        select.reshape(occ_shards * OWNED, NPAIR),
        spread.reshape(occ_shards, per * occ, OWNED),
    )


def share(x, axes, count):
    return lax.all_to_all(
        jnp.broadcast_to(x[None], (count,) + x.shape), axes, 0, 0, tiled=True
    )


def middle_kernel(q_local, dests, widths, b_ref, a_ref, *out_refs):
    step = pl.program_id(0)
    rows, b_local, v = b_ref.shape
    cwin = a_ref.shape[1] // NPAIR
    res = lax.dot_general(
        b_ref[...].reshape(rows * b_local, v),
        a_ref[...],
        (((1,), (0,)), ((), ())),
        preferred_element_type=jnp.float32,
    ).reshape(rows, b_local, cwin * NPAIR)
    q = step * rows + lax.broadcasted_iota(jnp.int32, (rows, 1, 1), 0)
    res = jnp.where(q < q_local, res, 0.0)
    res = jnp.swapaxes(res, 0, 1).astype(jnp.bfloat16)
    res = res.reshape(dests, sum(widths), rows, cwin * NPAIR)
    first = 0
    for out_ref, width in zip(out_refs, widths):
        for c in range(cwin):
            for h in range(width):
                out_ref[:, c, :, h * NPAIR : (h + 1) * NPAIR] = res[
                    :, first + h, :, c * NPAIR : (c + 1) * NPAIR
                ]
        first += width


def middle(factors, amps, dests, widths):
    q_local, b_local, v = factors.shape
    cwin = amps.shape[1] // NPAIR
    rows = 16
    width = sum(widths)
    return pl.pallas_call(
        functools.partial(middle_kernel, q_local, dests, widths),
        grid=(QPAD // rows,),
        in_specs=[
            pl.BlockSpec((rows, b_local, v), lambda s: (s, 0, 0)),
            pl.BlockSpec(amps.shape, lambda s: (0, 0)),
        ],
        out_specs=[
            pl.BlockSpec((dests, cwin, rows, w * NPAIR), lambda s: (0, 0, s, 0))
            for w in widths
        ],
        out_shape=[
            jax.ShapeDtypeStruct((dests, cwin, QPAD, w * NPAIR), jnp.bfloat16)
            for w in widths
        ],
        compiler_params=pltpu.CompilerParams(vmem_limit_bytes=48 << 20),
        cost_estimate=pl.CostEstimate(
            flops=2 * q_local * b_local * v * cwin * NPAIR,
            bytes_accessed=2 * (factors.size + dests * cwin * QPAD * width * NPAIR),
            transcendentals=0,
        ),
    )(factors, amps)


def column_kernel(at_ref, *refs):
    pieces, out_ref = refs[:-1], refs[-1]
    occ_at, core_at = at_ref[0], at_ref[1]
    count = len(pieces)
    a_part = pieces[0].shape[2]
    own = [ref[core_at] for ref in pieces]
    for p in range(count):
        k = lax.rem(occ_at - p + count, count)
        value = own[0]
        for n in range(1, count):
            value = jnp.where(k == n, own[n], value)
        out_ref[:, :, p * a_part : (p + 1) * a_part] = jnp.broadcast_to(
            value[None], (out_ref.shape[0],) + value.shape
        )


def column_copies(pieces, at, copies):
    _, depth, a_part = pieces[0].shape
    vmem = pl.BlockSpec(memory_space=pltpu.VMEM)
    return pl.pallas_call(
        column_kernel,
        in_specs=[pl.BlockSpec(memory_space=pltpu.SMEM)] + [vmem] * len(pieces),
        out_specs=vmem,
        out_shape=jax.ShapeDtypeStruct(
            (copies, depth, len(pieces) * a_part), jnp.bfloat16
        ),
        compiler_params=pltpu.CompilerParams(vmem_limit_bytes=16 << 20),
    )(at, *pieces)


def ladder_kernel(
    first, at_ref, own_ref, keep_ref, select_ref, m_hbm, far_hbm, *refs
):
    outs, (m_buf, far_buf, acc, sems) = refs[:-4], refs[-4:]
    _, sources, depth, lanes = m_buf.shape
    width = lanes // NPAIR
    steps = [(c, yl) for c in range(2) for yl in range(2)]
    tiles = [
        pltpu.make_async_copy(
            m_hbm.at[(at_ref[0] + yl) % 2, :, (at_ref[1] + c) % 2],
            m_buf.at[n],
            sems.at[n],
        )
        for n, (c, yl) in enumerate(steps)
    ]
    fars = [
        pltpu.make_async_copy(far_hbm.at[yl], far_buf.at[yl], sems.at[4 + yl])
        for yl in range(2)
    ]
    for copy in (tiles[0], tiles[1], fars[0], tiles[2], fars[1], tiles[3]):
        copy.start()
    for n, (c, yl) in enumerate(steps):
        tiles[n].wait()
        if c:
            fars[yl].wait()
        part = jnp.dot(
            (far_buf if c else own_ref)[yl],
            m_buf[n].reshape(sources * depth, lanes),
            preferred_element_type=jnp.float32,
        )
        acc[...] = part if n == 0 else acc[...] + part
    for h in range(width):
        part = acc[:, h * NPAIR : (h + 1) * NPAIR].astype(jnp.bfloat16)
        rows = lax.dot_general(
            select_ref[...],
            part,
            (((1,), (1,)), ((), ())),
            preferred_element_type=jnp.float32,
        )
        rows = (rows * keep_ref[first + h : first + h + 1, :]).astype(jnp.bfloat16)
        rows = rows.reshape(len(outs), OWNED, -1)
        for r, out in enumerate(outs):
            out[h] = rows[r]


def ladder_rows(first, tiles, own, far, keep, select, at):
    a_size = own.shape[1]
    lanes = tiles.shape[4]
    owners = select.shape[0] // OWNED
    out = jax.ShapeDtypeStruct((lanes // NPAIR, OWNED, a_size), jnp.bfloat16)
    vmem = pl.BlockSpec(memory_space=pltpu.VMEM)
    hbm = pl.BlockSpec(memory_space=pl.ANY)
    return pl.pallas_call(
        functools.partial(ladder_kernel, first),
        in_specs=[pl.BlockSpec(memory_space=pltpu.SMEM), vmem, vmem, vmem, hbm, hbm],
        out_specs=[vmem] * owners,
        out_shape=[out] * owners,
        scratch_shapes=[
            pltpu.VMEM((4, tiles.shape[1]) + tiles.shape[3:], jnp.bfloat16),
            pltpu.VMEM(far.shape, jnp.bfloat16),
            pltpu.VMEM((a_size, lanes), jnp.float32),
            pltpu.SemaphoreType.DMA((6,)),
        ],
        compiler_params=pltpu.CompilerParams(vmem_limit_bytes=24 << 20),
        cost_estimate=pl.CostEstimate(
            flops=2 * tiles.size * a_size,
            bytes_accessed=2 * (tiles.size + own.size + far.size),
            transcendentals=0,
        ),
    )(at, own, keep, select, tiles, far)


def unpack_kernel(widths, at_ref, spread_ref, *refs):
    parts, out_ref = refs[:-1], refs[-1]
    r = pl.program_id(0)
    occ_local, _, _, occ, a_size = out_ref.shape
    count = len(parts) // len(widths)

    def source(n):
        first = 0
        for k, width in enumerate(widths):
            for h in range(width):
                rows = jnp.dot(
                    spread_ref[at_ref[count]],
                    parts[k * count + n][h],
                    preferred_element_type=jnp.float32,
                ).astype(jnp.bfloat16)
                out_ref[:, 0, first + h] = rows.reshape(occ_local, occ, a_size)
            first += width

    for n in range(count):
        pl.when(r == n)(functools.partial(source, n))


def unpack(parts, spread, x_from, shape):
    occ_local, count, width, occ, a_size = shape
    vmem = pl.BlockSpec(memory_space=pltpu.VMEM)
    return pl.pallas_call(
        functools.partial(unpack_kernel, WIDTHS),
        grid_spec=pltpu.PrefetchScalarGridSpec(
            num_scalar_prefetch=1,
            grid=(count,),
            in_specs=[vmem] * (1 + len(parts)),
            out_specs=pl.BlockSpec(
                (occ_local, 1, width, occ, a_size), lambda r, at: (0, at[r], 0, 0, 0)
            ),
        ),
        out_shape=jax.ShapeDtypeStruct(shape, jnp.bfloat16),
        compiler_params=pltpu.CompilerParams(vmem_limit_bytes=16 << 20),
    )(x_from, spread, *parts)


def per_device(factors, amplitudes, block_sizes):
    q_local, b_local, v = factors.shape
    occ_local, occ, cwin, tile = amplitudes.shape
    occ_shards, shards = occ // occ_local, v // tile
    nx = lax.axis_size("x")
    width = tile // nx
    irreps = block_sizes.shape[0]
    block = v // irreps
    pick_np, select_np, spread_np = pair_tables(occ, cwin, occ_shards)
    occ_at, x_at, core_at = (lax.axis_index(n) for n in (OCC, "x", "core"))

    position = jnp.arange(v, dtype=jnp.int32)
    onehot = (position // block)[:, None] == jnp.arange(irreps, dtype=jnp.int32)[None, :]
    size_at = jnp.sum(jnp.where(onehot, block_sizes[None, :], 0), axis=1)
    usable = position % block < size_at

    own = jnp.transpose(amplitudes, (3, 2, 0, 1)).reshape(tile, cwin * occ_local * occ)
    core_swap = [(0, 1), (1, 0)]
    every = share(own, OCC + ("x", "yl", "z"), occ_shards * shards)
    every = every.reshape(occ_shards, v, cwin * occ_local * occ)
    antisym = jnp.einsum(
        "odl,olm->dm",
        every,
        jnp.asarray(pick_np, jnp.bfloat16),
        preferred_element_type=jnp.float32,
    )
    keep = usable[:, None] & jnp.repeat(usable[:cwin], NPAIR)[None, :]
    antisym = jnp.where(keep, antisym, 0.0).astype(jnp.bfloat16)

    cols = jnp.transpose(factors[:, :, :cwin], (2, 0, 1))
    cols = jnp.pad(cols, ((0, 0), (0, QPAD - q_local), (0, 0)))
    pieces = [cols]
    for k in range(1, occ_shards):
        shift = [(o, (o + k) % occ_shards) for o in range(occ_shards)]
        pieces.append(lax.ppermute(cols, OCC, shift))
    sources = shards // 2
    where = jnp.stack([occ_at, core_at]).astype(jnp.int32)
    half = column_copies(pieces, where, sources)
    half = lax.all_to_all(half, TILE[1:], 0, 0, tiled=True)
    half, mids = lax.optimization_barrier(
        (half, middle(factors, antisym, shards, WIDTHS))
    )
    half = half.reshape(sources * QPAD, v).T
    swap_y = [(0, 3), (3, 0), (1, 2), (2, 1)]
    other = lax.ppermute(half, ("yh", "yl"), swap_y)
    own_cols = jnp.stack([half, other])
    far_cols = lax.ppermute(own_cols, "core", core_swap)

    tile_at = lax.axis_index(("yl", "z"))
    b_first = occ_at * b_local + tile_at * tile + x_at * width
    usable_b = lax.dynamic_slice_in_dim(usable, b_first, width)
    outer = (usable_b[:, None] & usable[None, :]).astype(jnp.float32)
    outer = jnp.pad(outer, ((0, -width % 8), (0, 0)))
    select = jnp.asarray(np.concatenate([select_np, select_np]), jnp.bfloat16)
    select = lax.dynamic_slice_in_dim(select, x_at * OWNED, occ_shards * OWNED)
    spread = jnp.asarray(spread_np, jnp.bfloat16)
    at = jnp.stack([lax.axis_index("yl"), core_at]).astype(jnp.int32)

    shape = (occ_local, nx, width, occ, v)
    x_from = (occ_at - jnp.arange(nx, dtype=jnp.int32) + nx) % nx
    x_from = jnp.append(x_from, occ_at.astype(jnp.int32))
    first, tiles, parts, landed = 0, None, None, []
    for mid, w in zip(mids, WIDTHS):
        mid = mid.reshape(shards, cwin * QPAD, w * NPAIR)
        if tiles is not None:
            tiles, mid = lax.optimization_barrier((tiles, mid))
        tiles = lax.all_to_all(mid, TILE, 0, 0, tiled=True)
        if parts is not None:
            tiles, parts = lax.optimization_barrier((tiles, parts))
        parts = ladder_rows(
            first,
            tiles.reshape(2, sources, cwin, QPAD, w * NPAIR),
            own_cols, far_cols, outer, select, at,
        )
        if landed:
            landed, _ = lax.optimization_barrier((landed, parts))
        sent = {}
        for r in range(nx):
            perm = [
                (o * nx + x, ((x + r) % nx) * nx + o)
                for o in range(occ_shards)
                for x in range(nx)
            ]
            sent[r] = lax.ppermute(parts[r], OCC + ("x",), perm)
        landed += [sent[r] for r in range(nx)]
        first += w
    out = unpack(landed, spread, x_from, shape)
    out = out.reshape(occ_local, nx * width, occ, v)
    return jnp.transpose(out, (0, 2, 3, 1))


def solution(mesh):
    split = Mesh(
        mesh.devices.reshape(2, 2, 4, 2, 4), ("yh", "core", "x", "yl", "z")
    )
    virt = ("x", "yl", "z")
    return jax.shard_map(
        per_device,
        mesh=split,
        in_specs=(P(virt, OCC, None), P(OCC, None, None, virt), P()),
        out_specs=P(OCC, None, None, virt),
        check_vma=False,
    )
```

```python
import functools

import jax
import jax.numpy as jnp
import numpy as np
from jax import lax
from jax.experimental import pallas as pl
from jax.experimental.pallas import tpu as pltpu
from jax.sharding import Mesh, PartitionSpec as P

OCC = ("yh", "core")
TILE = ("yl", "z", "x")
NPAIR = 128
OWNED = 56
QPAD = 80
WIDTHS = (4, 1)


def pair_tables(occ, cwin, occ_shards):
    pairs = [(i, j) for i in range(occ) for j in range(i + 1, occ)]
    per = occ // occ_shards
    pick = np.zeros((occ_shards, cwin, per, occ, cwin, NPAIR), np.float32)
    select = np.zeros((occ_shards, OWNED, NPAIR), np.float32)
    spread = np.zeros((occ_shards, per, occ, OWNED), np.float32)
    count = [0] * occ_shards
    for p, (i, j) in enumerate(pairs):
        for c in range(cwin):
            pick[i // per, c, i % per, j, c, p] = 1.0
            pick[j // per, c, j % per, i, c, p] = -1.0
        for o in sorted({i // per, j // per}):
            n = count[o]
            count[o] += 1
            select[o, n, p] = 1.0
            if i // per == o:
                spread[o, i % per, j, n] = 1.0
            if j // per == o:
                spread[o, j % per, i, n] = -1.0
    return (
        pick.reshape(occ_shards, cwin * per * occ, cwin * NPAIR),
        select.reshape(occ_shards * OWNED, NPAIR),
        spread.reshape(occ_shards, per * occ, OWNED),
    )


def share(x, axes, count):
    return lax.all_to_all(
        jnp.broadcast_to(x[None], (count,) + x.shape), axes, 0, 0, tiled=True
    )


def middle_kernel(q_local, dests, widths, b_ref, a_ref, *out_refs):
    step = pl.program_id(0)
    rows, b_local, v = b_ref.shape
    cwin = a_ref.shape[1] // NPAIR
    res = lax.dot_general(
        b_ref[...].reshape(rows * b_local, v),
        a_ref[...],
        (((1,), (0,)), ((), ())),
        preferred_element_type=jnp.float32,
    ).reshape(rows, b_local, cwin * NPAIR)
    q = step * rows + lax.broadcasted_iota(jnp.int32, (rows, 1, 1), 0)
    res = jnp.where(q < q_local, res, 0.0)
    res = jnp.swapaxes(res, 0, 1).astype(jnp.bfloat16)
    res = res.reshape(dests, sum(widths), rows, cwin * NPAIR)
    first = 0
    for out_ref, width in zip(out_refs, widths):
        for c in range(cwin):
            for h in range(width):
                out_ref[:, c, :, h * NPAIR : (h + 1) * NPAIR] = res[
                    :, first + h, :, c * NPAIR : (c + 1) * NPAIR
                ]
        first += width


def middle(factors, amps, dests, widths):
    q_local, b_local, v = factors.shape
    cwin = amps.shape[1] // NPAIR
    rows = 16
    width = sum(widths)
    return pl.pallas_call(
        functools.partial(middle_kernel, q_local, dests, widths),
        grid=(QPAD // rows,),
        in_specs=[
            pl.BlockSpec((rows, b_local, v), lambda s: (s, 0, 0)),
            pl.BlockSpec(amps.shape, lambda s: (0, 0)),
        ],
        out_specs=[
            pl.BlockSpec((dests, cwin, rows, w * NPAIR), lambda s: (0, 0, s, 0))
            for w in widths
        ],
        out_shape=[
            jax.ShapeDtypeStruct((dests, cwin, QPAD, w * NPAIR), jnp.bfloat16)
            for w in widths
        ],
        compiler_params=pltpu.CompilerParams(vmem_limit_bytes=48 << 20),
        cost_estimate=pl.CostEstimate(
            flops=2 * q_local * b_local * v * cwin * NPAIR,
            bytes_accessed=2 * (factors.size + dests * cwin * QPAD * width * NPAIR),
            transcendentals=0,
        ),
    )(factors, amps)


def column_kernel(at_ref, *refs):
    pieces, out_ref = refs[:-1], refs[-1]
    occ_at, core_at = at_ref[0], at_ref[1]
    count = len(pieces)
    a_part = pieces[0].shape[2]
    own = [ref[core_at] for ref in pieces]
    for p in range(count):
        k = lax.rem(occ_at - p + count, count)
        value = own[0]
        for n in range(1, count):
            value = jnp.where(k == n, own[n], value)
        out_ref[:, :, p * a_part : (p + 1) * a_part] = jnp.broadcast_to(
            value[None], (out_ref.shape[0],) + value.shape
        )


def column_copies(pieces, at, copies):
    _, depth, a_part = pieces[0].shape
    vmem = pl.BlockSpec(memory_space=pltpu.VMEM)
    return pl.pallas_call(
        column_kernel,
        in_specs=[pl.BlockSpec(memory_space=pltpu.SMEM)] + [vmem] * len(pieces),
        out_specs=vmem,
        out_shape=jax.ShapeDtypeStruct(
            (copies, depth, len(pieces) * a_part), jnp.bfloat16
        ),
        compiler_params=pltpu.CompilerParams(vmem_limit_bytes=16 << 20),
    )(at, *pieces)


def ladder_kernel(
    first, at_ref, own_ref, keep_ref, select_ref, m_hbm, far_hbm, *refs
):
    outs, (m_buf, far_buf, acc, sems) = refs[:-4], refs[-4:]
    _, sources, depth, lanes = m_buf.shape
    width = lanes // NPAIR
    steps = [(c, yl) for c in range(2) for yl in range(2)]
    tiles = [
        pltpu.make_async_copy(
            m_hbm.at[(at_ref[0] + yl) % 2, :, (at_ref[1] + c) % 2],
            m_buf.at[n],
            sems.at[n],
        )
        for n, (c, yl) in enumerate(steps)
    ]
    fars = [
        pltpu.make_async_copy(far_hbm.at[yl], far_buf.at[yl], sems.at[4 + yl])
        for yl in range(2)
    ]
    for copy in (tiles[0], tiles[1], fars[0], tiles[2], fars[1], tiles[3]):
        copy.start()
    for n, (c, yl) in enumerate(steps):
        tiles[n].wait()
        if c:
            fars[yl].wait()
        part = jnp.dot(
            (far_buf if c else own_ref)[yl],
            m_buf[n].reshape(sources * depth, lanes),
            preferred_element_type=jnp.float32,
        )
        acc[...] = part if n == 0 else acc[...] + part
    for h in range(width):
        part = acc[:, h * NPAIR : (h + 1) * NPAIR].astype(jnp.bfloat16)
        rows = lax.dot_general(
            select_ref[...],
            part,
            (((1,), (1,)), ((), ())),
            preferred_element_type=jnp.float32,
        )
        rows = (rows * keep_ref[first + h : first + h + 1, :]).astype(jnp.bfloat16)
        rows = rows.reshape(len(outs), OWNED, -1)
        for r, out in enumerate(outs):
            out[h] = rows[r]


def ladder_rows(first, tiles, own, far, keep, select, at):
    a_size = own.shape[1]
    lanes = tiles.shape[4]
    owners = select.shape[0] // OWNED
    out = jax.ShapeDtypeStruct((lanes // NPAIR, OWNED, a_size), jnp.bfloat16)
    vmem = pl.BlockSpec(memory_space=pltpu.VMEM)
    hbm = pl.BlockSpec(memory_space=pl.ANY)
    return pl.pallas_call(
        functools.partial(ladder_kernel, first),
        in_specs=[pl.BlockSpec(memory_space=pltpu.SMEM), vmem, vmem, vmem, hbm, hbm],
        out_specs=[vmem] * owners,
        out_shape=[out] * owners,
        scratch_shapes=[
            pltpu.VMEM((4, tiles.shape[1]) + tiles.shape[3:], jnp.bfloat16),
            pltpu.VMEM(far.shape, jnp.bfloat16),
            pltpu.VMEM((a_size, lanes), jnp.float32),
            pltpu.SemaphoreType.DMA((6,)),
        ],
        compiler_params=pltpu.CompilerParams(vmem_limit_bytes=24 << 20),
        cost_estimate=pl.CostEstimate(
            flops=2 * tiles.size * a_size,
            bytes_accessed=2 * (tiles.size + own.size + far.size),
            transcendentals=0,
        ),
    )(at, own, keep, select, tiles, far)


def unpack_kernel(at_ref, spread_ref, *refs):
    out_ref = refs[-1]
    r = pl.program_id(0)
    occ_local, _, width, occ, a_size = out_ref.shape
    spread = spread_ref[at_ref[pl.num_programs(0)]]

    def source(part_ref):
        for h in range(width):
            rows = jnp.dot(spread, part_ref[h], preferred_element_type=jnp.float32)
            rows = rows.astype(jnp.bfloat16)
            out_ref[:, 0, h] = rows.reshape(occ_local, occ, a_size)

    for n in range(4):
        pl.when(r == n)(functools.partial(source, refs[n]))


def unpack(parts, spread, x_from, first, out, shape):
    occ_local, count, _, occ, a_size = shape
    width = parts[0].shape[0]
    vmem = pl.BlockSpec(memory_space=pltpu.VMEM)
    so_far = [] if out is None else [out]
    return pl.pallas_call(
        unpack_kernel,
        grid_spec=pltpu.PrefetchScalarGridSpec(
            num_scalar_prefetch=1,
            grid=(count,),
            in_specs=[vmem] * (1 + count)
            + [pl.BlockSpec(memory_space=pl.ANY)] * len(so_far),
            out_specs=pl.BlockSpec(
                (occ_local, 1, width, occ, a_size),
                lambda r, at: (0, at[r], first // width, 0, 0),
            ),
        ),
        out_shape=jax.ShapeDtypeStruct(shape, jnp.bfloat16),
        input_output_aliases={2 + count: 0} if so_far else {},
        compiler_params=pltpu.CompilerParams(vmem_limit_bytes=16 << 20),
    )(x_from, spread, *parts, *so_far)


def per_device(factors, amplitudes, block_sizes):
    q_local, b_local, v = factors.shape
    occ_local, occ, cwin, tile = amplitudes.shape
    occ_shards, shards = occ // occ_local, v // tile
    nx = lax.axis_size("x")
    width = tile // nx
    irreps = block_sizes.shape[0]
    block = v // irreps
    pick_np, select_np, spread_np = pair_tables(occ, cwin, occ_shards)
    occ_at, x_at, core_at = (lax.axis_index(n) for n in (OCC, "x", "core"))

    position = jnp.arange(v, dtype=jnp.int32)
    onehot = (position // block)[:, None] == jnp.arange(irreps, dtype=jnp.int32)[None, :]
    size_at = jnp.sum(jnp.where(onehot, block_sizes[None, :], 0), axis=1)
    usable = position % block < size_at

    own = jnp.transpose(amplitudes, (3, 2, 0, 1)).reshape(tile, cwin * occ_local * occ)
    core_swap = [(0, 1), (1, 0)]
    every = share(own, OCC + ("x", "yl", "z"), occ_shards * shards)
    every = every.reshape(occ_shards, v, cwin * occ_local * occ)
    antisym = jnp.einsum(
        "odl,olm->dm",
        every,
        jnp.asarray(pick_np, jnp.bfloat16),
        preferred_element_type=jnp.float32,
    )
    keep = usable[:, None] & jnp.repeat(usable[:cwin], NPAIR)[None, :]
    antisym = jnp.where(keep, antisym, 0.0).astype(jnp.bfloat16)

    cols = jnp.transpose(factors[:, :, :cwin], (2, 0, 1))
    cols = jnp.pad(cols, ((0, 0), (0, QPAD - q_local), (0, 0)))
    pieces = [cols]
    for k in range(1, occ_shards):
        shift = [(o, (o + k) % occ_shards) for o in range(occ_shards)]
        pieces.append(lax.ppermute(cols, OCC, shift))
    sources = shards // 2
    where = jnp.stack([occ_at, core_at]).astype(jnp.int32)
    half = column_copies(pieces, where, sources)
    half = lax.all_to_all(half, TILE[1:], 0, 0, tiled=True)
    half, mids = lax.optimization_barrier(
        (half, middle(factors, antisym, shards, WIDTHS))
    )
    half = half.reshape(sources * QPAD, v).T
    swap_y = [(0, 3), (3, 0), (1, 2), (2, 1)]
    other = lax.ppermute(half, ("yh", "yl"), swap_y)
    own_cols = jnp.stack([half, other])
    far_cols = lax.ppermute(own_cols, "core", core_swap)

    tile_at = lax.axis_index(("yl", "z"))
    b_first = occ_at * b_local + tile_at * tile + x_at * width
    usable_b = lax.dynamic_slice_in_dim(usable, b_first, width)
    outer = (usable_b[:, None] & usable[None, :]).astype(jnp.float32)
    outer = jnp.pad(outer, ((0, -width % 8), (0, 0)))
    select = jnp.asarray(np.concatenate([select_np, select_np]), jnp.bfloat16)
    select = lax.dynamic_slice_in_dim(select, x_at * OWNED, occ_shards * OWNED)
    spread = jnp.asarray(spread_np, jnp.bfloat16)
    at = jnp.stack([lax.axis_index("yl"), core_at]).astype(jnp.int32)

    shape = (occ_local, nx, width, occ, v)
    x_from = (occ_at - jnp.arange(nx, dtype=jnp.int32) + nx) % nx
    x_from = jnp.append(x_from, occ_at.astype(jnp.int32))
    first, tiles, parts, landed, out = 0, None, None, [], None
    for mid, w in zip(mids, WIDTHS):
        mid = mid.reshape(shards, cwin * QPAD, w * NPAIR)
        if tiles is not None:
            tiles, mid = lax.optimization_barrier((tiles, mid))
        tiles = lax.all_to_all(mid, TILE, 0, 0, tiled=True)
        if parts is not None:
            tiles, parts = lax.optimization_barrier((tiles, parts))
        parts = ladder_rows(
            first,
            tiles.reshape(2, sources, cwin, QPAD, w * NPAIR),
            own_cols, far_cols, outer, select, at,
        )
        if landed:
            landed, _ = lax.optimization_barrier((landed, parts))
            out = unpack(landed, spread, x_from, 0, out, shape)
        landed = []
        for r in range(nx):
            perm = [
                (o * nx + x, ((x + r) % nx) * nx + o)
                for o in range(occ_shards)
                for x in range(nx)
            ]
            landed.append(lax.ppermute(parts[r], OCC + ("x",), perm))
        first += w
    out = unpack(landed, spread, x_from, first - w, out, shape)
    out = out.reshape(occ_local, nx * width, occ, v)
    return jnp.transpose(out, (0, 2, 3, 1))


def solution(mesh):
    split = Mesh(
        mesh.devices.reshape(2, 2, 4, 2, 4), ("yh", "core", "x", "yl", "z")
    )
    virt = ("x", "yl", "z")
    return jax.shard_map(
        per_device,
        mesh=split,
        in_specs=(P(virt, OCC, None), P(OCC, None, None, virt), P()),
        out_specs=P(OCC, None, None, virt),
        check_vma=False,
    )
```

```python
import functools

import jax
import jax.numpy as jnp
import numpy as np
from jax import lax
from jax.experimental import pallas as pl
from jax.experimental.pallas import tpu as pltpu
from jax.sharding import Mesh, PartitionSpec as P

OCC = ("yh", "core")
TILE = ("yl", "z", "x")
NPAIR = 128
OWNED = 56
QPAD = 80
WIDTHS = (4, 1)


def pair_tables(occ, cwin, occ_shards):
    pairs = [(i, j) for i in range(occ) for j in range(i + 1, occ)]
    per = occ // occ_shards
    pick = np.zeros((occ_shards, cwin, per, occ, cwin, NPAIR), np.float32)
    select = np.zeros((occ_shards, OWNED, NPAIR), np.float32)
    spread = np.zeros((occ_shards, per, occ, OWNED), np.float32)
    count = [0] * occ_shards
    for p, (i, j) in enumerate(pairs):
        for c in range(cwin):
            pick[i // per, c, i % per, j, c, p] = 1.0
            pick[j // per, c, j % per, i, c, p] = -1.0
        for o in sorted({i // per, j // per}):
            n = count[o]
            count[o] += 1
            select[o, n, p] = 1.0
            if i // per == o:
                spread[o, i % per, j, n] = 1.0
            if j // per == o:
                spread[o, j % per, i, n] = -1.0
    return (
        pick.reshape(occ_shards, cwin * per * occ, cwin * NPAIR),
        select.reshape(occ_shards * OWNED, NPAIR),
        spread.reshape(occ_shards, per * occ, OWNED),
    )


def share(x, axes, count):
    return lax.all_to_all(
        jnp.broadcast_to(x[None], (count,) + x.shape), axes, 0, 0, tiled=True
    )


def middle_kernel(q_local, dests, widths, b_ref, a_ref, *out_refs):
    step = pl.program_id(0)
    rows, b_local, v = b_ref.shape
    cwin = a_ref.shape[1] // NPAIR
    res = lax.dot_general(
        b_ref[...].reshape(rows * b_local, v),
        a_ref[...],
        (((1,), (0,)), ((), ())),
        preferred_element_type=jnp.float32,
    ).reshape(rows, b_local, cwin * NPAIR)
    q = step * rows + lax.broadcasted_iota(jnp.int32, (rows, 1, 1), 0)
    res = jnp.where(q < q_local, res, 0.0)
    res = jnp.swapaxes(res, 0, 1).astype(jnp.bfloat16)
    res = res.reshape(dests, sum(widths), rows, cwin * NPAIR)
    first = 0
    for out_ref, width in zip(out_refs, widths):
        for c in range(cwin):
            for h in range(width):
                out_ref[:, c, :, h * NPAIR : (h + 1) * NPAIR] = res[
                    :, first + h, :, c * NPAIR : (c + 1) * NPAIR
                ]
        first += width


def middle(factors, amps, dests, widths):
    q_local, b_local, v = factors.shape
    cwin = amps.shape[1] // NPAIR
    rows = 16
    width = sum(widths)
    return pl.pallas_call(
        functools.partial(middle_kernel, q_local, dests, widths),
        grid=(QPAD // rows,),
        in_specs=[
            pl.BlockSpec((rows, b_local, v), lambda s: (s, 0, 0)),
            pl.BlockSpec(amps.shape, lambda s: (0, 0)),
        ],
        out_specs=[
            pl.BlockSpec((dests, cwin, rows, w * NPAIR), lambda s: (0, 0, s, 0))
            for w in widths
        ],
        out_shape=[
            jax.ShapeDtypeStruct((dests, cwin, QPAD, w * NPAIR), jnp.bfloat16)
            for w in widths
        ],
        compiler_params=pltpu.CompilerParams(vmem_limit_bytes=48 << 20),
        cost_estimate=pl.CostEstimate(
            flops=2 * q_local * b_local * v * cwin * NPAIR,
            bytes_accessed=2 * (factors.size + dests * cwin * QPAD * width * NPAIR),
            transcendentals=0,
        ),
    )(factors, amps)


def column_kernel(at_ref, *refs):
    pieces, out_ref = refs[:-1], refs[-1]
    occ_at, core_at = at_ref[0], at_ref[1]
    count = len(pieces)
    a_part = pieces[0].shape[2]
    own = [ref[core_at] for ref in pieces]
    for p in range(count):
        k = lax.rem(occ_at - p + count, count)
        value = own[0]
        for n in range(1, count):
            value = jnp.where(k == n, own[n], value)
        out_ref[:, :, p * a_part : (p + 1) * a_part] = jnp.broadcast_to(
            value[None], (out_ref.shape[0],) + value.shape
        )


def column_copies(pieces, at, copies):
    _, depth, a_part = pieces[0].shape
    vmem = pl.BlockSpec(memory_space=pltpu.VMEM)
    return pl.pallas_call(
        column_kernel,
        in_specs=[pl.BlockSpec(memory_space=pltpu.SMEM)] + [vmem] * len(pieces),
        out_specs=vmem,
        out_shape=jax.ShapeDtypeStruct(
            (copies, depth, len(pieces) * a_part), jnp.bfloat16
        ),
        compiler_params=pltpu.CompilerParams(vmem_limit_bytes=16 << 20),
    )(at, *pieces)


def ladder_kernel(
    first, at_ref, own_ref, keep_ref, select_ref, m_hbm, far_hbm, *refs
):
    outs, (m_buf, far_buf, acc, sems) = refs[:-4], refs[-4:]
    _, sources, depth, lanes = m_buf.shape
    width = lanes // NPAIR
    steps = [(c, yl) for c in range(2) for yl in range(2)]
    tiles = [
        pltpu.make_async_copy(
            m_hbm.at[(at_ref[0] + yl) % 2, :, (at_ref[1] + c) % 2],
            m_buf.at[n],
            sems.at[n],
        )
        for n, (c, yl) in enumerate(steps)
    ]
    fars = [
        pltpu.make_async_copy(far_hbm.at[yl], far_buf.at[yl], sems.at[4 + yl])
        for yl in range(2)
    ]
    for copy in (tiles[0], tiles[1], fars[0], tiles[2], fars[1], tiles[3]):
        copy.start()
    for n, (c, yl) in enumerate(steps):
        tiles[n].wait()
        if c:
            fars[yl].wait()
        part = jnp.dot(
            (far_buf if c else own_ref)[yl],
            m_buf[n].reshape(sources * depth, lanes),
            preferred_element_type=jnp.float32,
        )
        acc[...] = part if n == 0 else acc[...] + part
    for h in range(width):
        part = acc[:, h * NPAIR : (h + 1) * NPAIR].astype(jnp.bfloat16)
        rows = lax.dot_general(
            select_ref[...],
            part,
            (((1,), (1,)), ((), ())),
            preferred_element_type=jnp.float32,
        )
        rows = (rows * keep_ref[first + h : first + h + 1, :]).astype(jnp.bfloat16)
        rows = rows.reshape(len(outs), OWNED, -1)
        for r, out in enumerate(outs):
            out[h] = rows[r]


def ladder_rows(first, tiles, own, far, keep, select, at):
    a_size = own.shape[1]
    lanes = tiles.shape[4]
    owners = select.shape[0] // OWNED
    out = jax.ShapeDtypeStruct((lanes // NPAIR, OWNED, a_size), jnp.bfloat16)
    vmem = pl.BlockSpec(memory_space=pltpu.VMEM)
    hbm = pl.BlockSpec(memory_space=pl.ANY)
    return pl.pallas_call(
        functools.partial(ladder_kernel, first),
        in_specs=[pl.BlockSpec(memory_space=pltpu.SMEM), vmem, vmem, vmem, hbm, hbm],
        out_specs=[vmem] * owners,
        out_shape=[out] * owners,
        scratch_shapes=[
            pltpu.VMEM((4, tiles.shape[1]) + tiles.shape[3:], jnp.bfloat16),
            pltpu.VMEM(far.shape, jnp.bfloat16),
            pltpu.VMEM((a_size, lanes), jnp.float32),
            pltpu.SemaphoreType.DMA((6,)),
        ],
        compiler_params=pltpu.CompilerParams(vmem_limit_bytes=24 << 20),
        cost_estimate=pl.CostEstimate(
            flops=2 * tiles.size * a_size,
            bytes_accessed=2 * (tiles.size + own.size + far.size),
            transcendentals=0,
        ),
    )(at, own, keep, select, tiles, far)


def unpack_kernel(first, at_ref, spread_ref, *refs):
    out_hbm, buf, sems = refs[-3:]
    count, occ_local, width, occ, a_size = buf.shape
    spread = spread_ref[at_ref[count]]
    copies = []
    for r in range(count):
        for h in range(width):
            rows = jnp.dot(spread, refs[r][h], preferred_element_type=jnp.float32)
            rows = rows.astype(jnp.bfloat16)
            buf[r, :, h] = rows.reshape(occ_local, occ, a_size)
        copies.append(
            pltpu.make_async_copy(
                buf.at[r],
                out_hbm.at[:, at_ref[r], pl.ds(first, width)],
                sems.at[r],
            )
        )
        copies[r].start()
    for copy in copies:
        copy.wait()


def unpack(parts, spread, x_from, first, out, shape):
    occ_local, count, _, occ, a_size = shape
    width = parts[0].shape[0]
    vmem = pl.BlockSpec(memory_space=pltpu.VMEM)
    hbm = pl.BlockSpec(memory_space=pl.ANY)
    so_far = [] if out is None else [out]
    return pl.pallas_call(
        functools.partial(unpack_kernel, first),
        in_specs=[pl.BlockSpec(memory_space=pltpu.SMEM)]
        + [vmem] * (1 + count)
        + [hbm] * len(so_far),
        out_specs=hbm,
        out_shape=jax.ShapeDtypeStruct(shape, jnp.bfloat16),
        scratch_shapes=[
            pltpu.VMEM((count, occ_local, width, occ, a_size), jnp.bfloat16),
            pltpu.SemaphoreType.DMA((count,)),
        ],
        input_output_aliases={2 + count: 0} if so_far else {},
        compiler_params=pltpu.CompilerParams(vmem_limit_bytes=16 << 20),
    )(x_from, spread, *parts, *so_far)


def per_device(factors, amplitudes, block_sizes):
    q_local, b_local, v = factors.shape
    occ_local, occ, cwin, tile = amplitudes.shape
    occ_shards, shards = occ // occ_local, v // tile
    nx = lax.axis_size("x")
    width = tile // nx
    irreps = block_sizes.shape[0]
    block = v // irreps
    pick_np, select_np, spread_np = pair_tables(occ, cwin, occ_shards)
    occ_at, x_at, core_at = (lax.axis_index(n) for n in (OCC, "x", "core"))

    position = jnp.arange(v, dtype=jnp.int32)
    onehot = (position // block)[:, None] == jnp.arange(irreps, dtype=jnp.int32)[None, :]
    size_at = jnp.sum(jnp.where(onehot, block_sizes[None, :], 0), axis=1)
    usable = position % block < size_at

    own = jnp.transpose(amplitudes, (3, 2, 0, 1)).reshape(tile, cwin * occ_local * occ)
    core_swap = [(0, 1), (1, 0)]
    every = share(own, OCC + ("x", "yl", "z"), occ_shards * shards)
    every = every.reshape(occ_shards, v, cwin * occ_local * occ)
    antisym = jnp.einsum(
        "odl,olm->dm",
        every,
        jnp.asarray(pick_np, jnp.bfloat16),
        preferred_element_type=jnp.float32,
    )
    keep = usable[:, None] & jnp.repeat(usable[:cwin], NPAIR)[None, :]
    antisym = jnp.where(keep, antisym, 0.0).astype(jnp.bfloat16)

    cols = jnp.transpose(factors[:, :, :cwin], (2, 0, 1))
    cols = jnp.pad(cols, ((0, 0), (0, QPAD - q_local), (0, 0)))
    pieces = [cols]
    for k in range(1, occ_shards):
        shift = [(o, (o + k) % occ_shards) for o in range(occ_shards)]
        pieces.append(lax.ppermute(cols, OCC, shift))
    sources = shards // 2
    where = jnp.stack([occ_at, core_at]).astype(jnp.int32)
    half = column_copies(pieces, where, sources)
    half = lax.all_to_all(half, TILE[1:], 0, 0, tiled=True)
    half, mids = lax.optimization_barrier(
        (half, middle(factors, antisym, shards, WIDTHS))
    )
    half = half.reshape(sources * QPAD, v).T
    swap_y = [(0, 3), (3, 0), (1, 2), (2, 1)]
    other = lax.ppermute(half, ("yh", "yl"), swap_y)
    own_cols = jnp.stack([half, other])
    far_cols = lax.ppermute(own_cols, "core", core_swap)

    tile_at = lax.axis_index(("yl", "z"))
    b_first = occ_at * b_local + tile_at * tile + x_at * width
    usable_b = lax.dynamic_slice_in_dim(usable, b_first, width)
    outer = (usable_b[:, None] & usable[None, :]).astype(jnp.float32)
    outer = jnp.pad(outer, ((0, -width % 8), (0, 0)))
    select = jnp.asarray(np.concatenate([select_np, select_np]), jnp.bfloat16)
    select = lax.dynamic_slice_in_dim(select, x_at * OWNED, occ_shards * OWNED)
    spread = jnp.asarray(spread_np, jnp.bfloat16)
    at = jnp.stack([lax.axis_index("yl"), core_at]).astype(jnp.int32)

    shape = (occ_local, nx, width, occ, v)
    x_from = (occ_at - jnp.arange(nx, dtype=jnp.int32) + nx) % nx
    x_from = jnp.append(x_from, occ_at.astype(jnp.int32))
    first, tiles, parts, landed, out = 0, None, None, [], None
    for mid, w in zip(mids, WIDTHS):
        mid = mid.reshape(shards, cwin * QPAD, w * NPAIR)
        if tiles is not None:
            tiles, mid = lax.optimization_barrier((tiles, mid))
        tiles = lax.all_to_all(mid, TILE, 0, 0, tiled=True)
        if parts is not None:
            tiles, parts = lax.optimization_barrier((tiles, parts))
        parts = ladder_rows(
            first,
            tiles.reshape(2, sources, cwin, QPAD, w * NPAIR),
            own_cols, far_cols, outer, select, at,
        )
        if landed:
            landed, _ = lax.optimization_barrier((landed, parts))
            out = unpack(landed, spread, x_from, 0, out, shape)
        landed = []
        for r in range(nx):
            perm = [
                (o * nx + x, ((x + r) % nx) * nx + o)
                for o in range(occ_shards)
                for x in range(nx)
            ]
            landed.append(lax.ppermute(parts[r], OCC + ("x",), perm))
        first += w
    out = unpack(landed, spread, x_from, first - w, out, shape)
    out = out.reshape(occ_local, nx * width, occ, v)
    return jnp.transpose(out, (0, 2, 3, 1))


def solution(mesh):
    split = Mesh(
        mesh.devices.reshape(2, 2, 4, 2, 4), ("yh", "core", "x", "yl", "z")
    )
    virt = ("x", "yl", "z")
    return jax.shard_map(
        per_device,
        mesh=split,
        in_specs=(P(virt, OCC, None), P(OCC, None, None, virt), P()),
        out_specs=P(OCC, None, None, virt),
        check_vma=False,
    )
```

```python
import functools

import jax
import jax.numpy as jnp
import numpy as np
from jax import lax
from jax.experimental import pallas as pl
from jax.experimental.pallas import tpu as pltpu
from jax.sharding import Mesh, PartitionSpec as P

OCC = ("yh", "core")
TILE = ("yl", "z", "x")
NPAIR = 128
OWNED = 56
QPAD = 80
WIDTHS = (4, 1)


def pair_tables(occ, cwin, occ_shards):
    pairs = [(i, j) for i in range(occ) for j in range(i + 1, occ)]
    per = occ // occ_shards
    pick = np.zeros((occ_shards, cwin, per, occ, cwin, NPAIR), np.float32)
    select = np.zeros((occ_shards, OWNED, NPAIR), np.float32)
    spread = np.zeros((occ_shards, per, occ, OWNED), np.float32)
    count = [0] * occ_shards
    for p, (i, j) in enumerate(pairs):
        for c in range(cwin):
            pick[i // per, c, i % per, j, c, p] = 1.0
            pick[j // per, c, j % per, i, c, p] = -1.0
        for o in sorted({i // per, j // per}):
            n = count[o]
            count[o] += 1
            select[o, n, p] = 1.0
            if i // per == o:
                spread[o, i % per, j, n] = 1.0
            if j // per == o:
                spread[o, j % per, i, n] = -1.0
    return (
        pick.reshape(occ_shards, cwin * per * occ, cwin * NPAIR),
        select.reshape(occ_shards * OWNED, NPAIR),
        spread.reshape(occ_shards, per * occ, OWNED),
    )


def share(x, axes, count):
    return lax.all_to_all(
        jnp.broadcast_to(x[None], (count,) + x.shape), axes, 0, 0, tiled=True
    )


def middle_kernel(q_local, dests, widths, b_ref, a_ref, *out_refs):
    step = pl.program_id(0)
    rows, b_local, v = b_ref.shape
    cwin = a_ref.shape[1] // NPAIR
    res = lax.dot_general(
        b_ref[...].reshape(rows * b_local, v),
        a_ref[...],
        (((1,), (0,)), ((), ())),
        preferred_element_type=jnp.float32,
    ).reshape(rows, b_local, cwin * NPAIR)
    q = step * rows + lax.broadcasted_iota(jnp.int32, (rows, 1, 1), 0)
    res = jnp.where(q < q_local, res, 0.0)
    res = jnp.swapaxes(res, 0, 1).astype(jnp.bfloat16)
    res = res.reshape(dests, sum(widths), rows, cwin * NPAIR)
    first = 0
    for out_ref, width in zip(out_refs, widths):
        for c in range(cwin):
            for h in range(width):
                out_ref[:, c, :, h * NPAIR : (h + 1) * NPAIR] = res[
                    :, first + h, :, c * NPAIR : (c + 1) * NPAIR
                ]
        first += width


def middle(factors, amps, dests, widths):
    q_local, b_local, v = factors.shape
    cwin = amps.shape[1] // NPAIR
    rows = 16
    width = sum(widths)
    return pl.pallas_call(
        functools.partial(middle_kernel, q_local, dests, widths),
        grid=(QPAD // rows,),
        in_specs=[
            pl.BlockSpec((rows, b_local, v), lambda s: (s, 0, 0)),
            pl.BlockSpec(amps.shape, lambda s: (0, 0)),
        ],
        out_specs=[
            pl.BlockSpec((dests, cwin, rows, w * NPAIR), lambda s: (0, 0, s, 0))
            for w in widths
        ],
        out_shape=[
            jax.ShapeDtypeStruct((dests, cwin, QPAD, w * NPAIR), jnp.bfloat16)
            for w in widths
        ],
        compiler_params=pltpu.CompilerParams(vmem_limit_bytes=48 << 20),
        cost_estimate=pl.CostEstimate(
            flops=2 * q_local * b_local * v * cwin * NPAIR,
            bytes_accessed=2 * (factors.size + dests * cwin * QPAD * width * NPAIR),
            transcendentals=0,
        ),
    )(factors, amps)


def column_kernel(at_ref, *refs):
    pieces, out_ref = refs[:-1], refs[-1]
    occ_at, core_at = at_ref[0], at_ref[1]
    count = len(pieces)
    a_part = pieces[0].shape[2]
    own = [ref[core_at] for ref in pieces]
    for p in range(count):
        k = lax.rem(occ_at - p + count, count)
        value = own[0]
        for n in range(1, count):
            value = jnp.where(k == n, own[n], value)
        out_ref[:, :, p * a_part : (p + 1) * a_part] = jnp.broadcast_to(
            value[None], (out_ref.shape[0],) + value.shape
        )


def column_copies(pieces, at, copies):
    _, depth, a_part = pieces[0].shape
    vmem = pl.BlockSpec(memory_space=pltpu.VMEM)
    return pl.pallas_call(
        column_kernel,
        in_specs=[pl.BlockSpec(memory_space=pltpu.SMEM)] + [vmem] * len(pieces),
        out_specs=vmem,
        out_shape=jax.ShapeDtypeStruct(
            (copies, depth, len(pieces) * a_part), jnp.bfloat16
        ),
        compiler_params=pltpu.CompilerParams(vmem_limit_bytes=16 << 20),
    )(at, *pieces)


def ladder_kernel(
    first, at_ref, own_ref, keep_ref, select_ref, m_hbm, far_hbm, *refs
):
    outs, (m_buf, far_buf, acc, sems) = refs[:-4], refs[-4:]
    _, sources, depth, lanes = m_buf.shape
    width = lanes // NPAIR
    steps = [(c, yl) for c in range(2) for yl in range(2)]
    tiles = [
        pltpu.make_async_copy(
            m_hbm.at[(at_ref[0] + yl) % 2, :, (at_ref[1] + c) % 2],
            m_buf.at[n],
            sems.at[n],
        )
        for n, (c, yl) in enumerate(steps)
    ]
    fars = [
        pltpu.make_async_copy(far_hbm.at[yl], far_buf.at[yl], sems.at[4 + yl])
        for yl in range(2)
    ]
    for copy in (tiles[0], tiles[1], fars[0], tiles[2], fars[1], tiles[3]):
        copy.start()
    for c in range(2):
        tiles[2 * c].wait()
        tiles[2 * c + 1].wait()
        if c:
            fars[0].wait()
            fars[1].wait()
        w = far_buf if c else own_ref
        part = jnp.dot(
            jnp.concatenate([w[0], w[1]], axis=1),
            m_buf[2 * c : 2 * c + 2].reshape(2 * sources * depth, lanes),
            preferred_element_type=jnp.float32,
        )
        acc[...] = part if c == 0 else acc[...] + part
    for h in range(width):
        part = acc[:, h * NPAIR : (h + 1) * NPAIR].astype(jnp.bfloat16)
        rows = lax.dot_general(
            select_ref[...],
            part,
            (((1,), (1,)), ((), ())),
            preferred_element_type=jnp.float32,
        )
        rows = (rows * keep_ref[first + h : first + h + 1, :]).astype(jnp.bfloat16)
        rows = rows.reshape(len(outs), OWNED, -1)
        for r, out in enumerate(outs):
            out[h] = rows[r]


def ladder_rows(first, tiles, own, far, keep, select, at):
    a_size = own.shape[1]
    lanes = tiles.shape[4]
    owners = select.shape[0] // OWNED
    out = jax.ShapeDtypeStruct((lanes // NPAIR, OWNED, a_size), jnp.bfloat16)
    vmem = pl.BlockSpec(memory_space=pltpu.VMEM)
    hbm = pl.BlockSpec(memory_space=pl.ANY)
    return pl.pallas_call(
        functools.partial(ladder_kernel, first),
        in_specs=[pl.BlockSpec(memory_space=pltpu.SMEM), vmem, vmem, vmem, hbm, hbm],
        out_specs=[vmem] * owners,
        out_shape=[out] * owners,
        scratch_shapes=[
            pltpu.VMEM((4, tiles.shape[1]) + tiles.shape[3:], jnp.bfloat16),
            pltpu.VMEM(far.shape, jnp.bfloat16),
            pltpu.VMEM((a_size, lanes), jnp.float32),
            pltpu.SemaphoreType.DMA((6,)),
        ],
        compiler_params=pltpu.CompilerParams(vmem_limit_bytes=24 << 20),
        cost_estimate=pl.CostEstimate(
            flops=2 * tiles.size * a_size,
            bytes_accessed=2 * (tiles.size + own.size + far.size),
            transcendentals=0,
        ),
    )(at, own, keep, select, tiles, far)


def unpack_kernel(first, at_ref, spread_ref, *refs):
    out_hbm, buf, sems = refs[-3:]
    count, occ_local, width, occ, a_size = buf.shape
    spread = spread_ref[at_ref[count]]
    copies = []
    for r in range(count):
        for h in range(width):
            rows = jnp.dot(spread, refs[r][h], preferred_element_type=jnp.float32)
            rows = rows.astype(jnp.bfloat16)
            buf[r, :, h] = rows.reshape(occ_local, occ, a_size)
        copies.append(
            pltpu.make_async_copy(
                buf.at[r],
                out_hbm.at[:, at_ref[r], pl.ds(first, width)],
                sems.at[r],
            )
        )
        copies[r].start()
    for copy in copies:
        copy.wait()


def unpack(parts, spread, x_from, first, out, shape):
    occ_local, count, _, occ, a_size = shape
    width = parts[0].shape[0]
    vmem = pl.BlockSpec(memory_space=pltpu.VMEM)
    hbm = pl.BlockSpec(memory_space=pl.ANY)
    so_far = [] if out is None else [out]
    return pl.pallas_call(
        functools.partial(unpack_kernel, first),
        in_specs=[pl.BlockSpec(memory_space=pltpu.SMEM)]
        + [vmem] * (1 + count)
        + [hbm] * len(so_far),
        out_specs=hbm,
        out_shape=jax.ShapeDtypeStruct(shape, jnp.bfloat16),
        scratch_shapes=[
            pltpu.VMEM((count, occ_local, width, occ, a_size), jnp.bfloat16),
            pltpu.SemaphoreType.DMA((count,)),
        ],
        input_output_aliases={2 + count: 0} if so_far else {},
        compiler_params=pltpu.CompilerParams(vmem_limit_bytes=16 << 20),
    )(x_from, spread, *parts, *so_far)


def per_device(factors, amplitudes, block_sizes):
    q_local, b_local, v = factors.shape
    occ_local, occ, cwin, tile = amplitudes.shape
    occ_shards, shards = occ // occ_local, v // tile
    nx = lax.axis_size("x")
    width = tile // nx
    irreps = block_sizes.shape[0]
    block = v // irreps
    pick_np, select_np, spread_np = pair_tables(occ, cwin, occ_shards)
    occ_at, x_at, core_at = (lax.axis_index(n) for n in (OCC, "x", "core"))

    position = jnp.arange(v, dtype=jnp.int32)
    onehot = (position // block)[:, None] == jnp.arange(irreps, dtype=jnp.int32)[None, :]
    size_at = jnp.sum(jnp.where(onehot, block_sizes[None, :], 0), axis=1)
    usable = position % block < size_at

    own = jnp.transpose(amplitudes, (3, 2, 0, 1)).reshape(tile, cwin * occ_local * occ)
    core_swap = [(0, 1), (1, 0)]
    every = share(own, OCC + ("x", "yl", "z"), occ_shards * shards)
    every = every.reshape(occ_shards, v, cwin * occ_local * occ)
    antisym = jnp.einsum(
        "odl,olm->dm",
        every,
        jnp.asarray(pick_np, jnp.bfloat16),
        preferred_element_type=jnp.float32,
    )
    keep = usable[:, None] & jnp.repeat(usable[:cwin], NPAIR)[None, :]
    antisym = jnp.where(keep, antisym, 0.0).astype(jnp.bfloat16)

    cols = jnp.transpose(factors[:, :, :cwin], (2, 0, 1))
    cols = jnp.pad(cols, ((0, 0), (0, QPAD - q_local), (0, 0)))
    pieces = [cols]
    for k in range(1, occ_shards):
        shift = [(o, (o + k) % occ_shards) for o in range(occ_shards)]
        pieces.append(lax.ppermute(cols, OCC, shift))
    sources = shards // 2
    where = jnp.stack([occ_at, core_at]).astype(jnp.int32)
    half = column_copies(pieces, where, sources)
    half = lax.all_to_all(half, TILE[1:], 0, 0, tiled=True)
    half, mids = lax.optimization_barrier(
        (half, middle(factors, antisym, shards, WIDTHS))
    )
    half = half.reshape(sources * QPAD, v).T
    swap_y = [(0, 3), (3, 0), (1, 2), (2, 1)]
    other = lax.ppermute(half, ("yh", "yl"), swap_y)
    own_cols = jnp.stack([half, other])
    far_cols = lax.ppermute(own_cols, "core", core_swap)

    tile_at = lax.axis_index(("yl", "z"))
    b_first = occ_at * b_local + tile_at * tile + x_at * width
    usable_b = lax.dynamic_slice_in_dim(usable, b_first, width)
    outer = (usable_b[:, None] & usable[None, :]).astype(jnp.float32)
    outer = jnp.pad(outer, ((0, -width % 8), (0, 0)))
    select = jnp.asarray(np.concatenate([select_np, select_np]), jnp.bfloat16)
    select = lax.dynamic_slice_in_dim(select, x_at * OWNED, occ_shards * OWNED)
    spread = jnp.asarray(spread_np, jnp.bfloat16)
    at = jnp.stack([lax.axis_index("yl"), core_at]).astype(jnp.int32)

    shape = (occ_local, nx, width, occ, v)
    x_from = (occ_at - jnp.arange(nx, dtype=jnp.int32) + nx) % nx
    x_from = jnp.append(x_from, occ_at.astype(jnp.int32))
    first, tiles, parts, landed, out = 0, None, None, [], None
    for mid, w in zip(mids, WIDTHS):
        mid = mid.reshape(shards, cwin * QPAD, w * NPAIR)
        if tiles is not None:
            tiles, mid = lax.optimization_barrier((tiles, mid))
        tiles = lax.all_to_all(mid, TILE, 0, 0, tiled=True)
        if parts is not None:
            tiles, parts = lax.optimization_barrier((tiles, parts))
        parts = ladder_rows(
            first,
            tiles.reshape(2, sources, cwin, QPAD, w * NPAIR),
            own_cols, far_cols, outer, select, at,
        )
        if landed:
            landed, _ = lax.optimization_barrier((landed, parts))
            out = unpack(landed, spread, x_from, 0, out, shape)
        landed = []
        for r in range(nx):
            perm = [
                (o * nx + x, ((x + r) % nx) * nx + o)
                for o in range(occ_shards)
                for x in range(nx)
            ]
            landed.append(lax.ppermute(parts[r], OCC + ("x",), perm))
        first += w
    out = unpack(landed, spread, x_from, first - w, out, shape)
    out = out.reshape(occ_local, nx * width, occ, v)
    return jnp.transpose(out, (0, 2, 3, 1))


def solution(mesh):
    split = Mesh(
        mesh.devices.reshape(2, 2, 4, 2, 4), ("yh", "core", "x", "yl", "z")
    )
    virt = ("x", "yl", "z")
    return jax.shard_map(
        per_device,
        mesh=split,
        in_specs=(P(virt, OCC, None), P(OCC, None, None, virt), P()),
        out_specs=P(OCC, None, None, virt),
        check_vma=False,
    )
```
